256 devices in a mesh: tile: 64 (over z, x, core), ka: 4 (over y).
Axes of the slice: x: 4, y: 4, z: 8, core: 2. Of those that a mesh axis runs over, the one named last changes fastest.
Arguments:
- amplitudes: bfloat16 [1024, 256, 512], P(('tile', 'ka')), may hold values from -6 to 6
- integrals: bfloat16 [512, 512, 4096], P('tile', None, 'ka'), may hold values from -0.015625 to 0.015625
- slot_block: int32 [512], replicated, may hold values from 0 to 256, as said below
- rest: bfloat16 [1024, 4096], P('tile', 'ka'), may hold values from -12 to 12
- occ_energy: float32 [1024], P('tile'), may hold values from -2 to -0.5
- vir_energy: float32 [4096], P('ka'), may hold values from 0.5 to 3
Outputs:
- new_amp: bfloat16 [1024, 4096], P('tile', 'ka')
The draws below stay inside these ranges and needn't reach their ends.
Inputs may be any that keep to these rules, and one draw needn't show every extreme that they name: `slot_block`: each of the 256 blocks is stored in exactly one slot; the value 256 marks an empty slot. Slots s*8 to s*8 + 7 belong to owner s along tile; an owner holds 0 to 8 blocks, and some owner holds exactly 8.
All inputs are finite; a program needn't handle non-finite values.
Results may differ from the reference program's by a relative error of at most 0.001.
Values may be sent and summed in bfloat16 or wider, within the bound.
No kernel may reach another device: no remote copies, remote signals or barrier semaphores. Data moves between devices by JAX's collectives and lax.ppermute only.
A program may use at most 128 MiB of HBM per device.

```python
import jax
import jax.numpy as jnp
from jax import lax

BW = 512
CAP = 8
NBLK = 256
SLOTS = 512
ROWS = 1024
PAIRS = 4096


def draw_slot_block(key, part):
    tile_count = SLOTS // CAP
    half_count = tile_count // 2
    sub_keys = jax.random.split(key, 4)
    firsts = jax.random.randint(sub_keys[0], (half_count,), 0, CAP + 1)
    firsts = firsts.at[0].set(CAP)
    counts = jnp.concatenate([firsts, CAP - firsts])
    counts = counts[jax.random.permutation(sub_keys[1], tile_count)]
    orders = jax.vmap(lambda sub_key: jax.random.permutation(sub_key, CAP))(jax.random.split(sub_keys[2], tile_count))
    is_live = (orders < counts[:, None]).reshape(-1)
    live_rank = jnp.cumsum(is_live.astype(jnp.int32)) - 1
    block_ids = jax.random.permutation(sub_keys[3], NBLK).astype(jnp.int32)
    chosen = block_ids[jnp.clip(live_rank, 0, NBLK - 1)]
    return jnp.where(is_live, chosen, NBLK).astype(jnp.int32)


def shard_levels(key, extent, pieces, least, high):
    gain, own = 1.0, jax.random.fold_in(key, 6)
    for dim, blocks in pieces:
        draws = jnp.exp(jax.random.uniform(jax.random.fold_in(own, dim), (blocks,), jnp.float32, least / len(pieces), high / len(pieces)))
        gain = gain * jnp.repeat(draws, extent[dim] // blocks).reshape([-1 if axis == dim else 1 for axis in range(len(extent))])
    return gain


def noise(key, shape, deviation, most, pieces=(), kind=jnp.bfloat16):
    gain = shard_levels(key, shape, pieces, -0.22, 0.18) if pieces else 1.0
    array = jax.random.normal(key, shape, jnp.float32) * deviation * gain
    return jnp.minimum(jnp.maximum(array, -most), most).astype(kind)


def setup_inputs(seed: int = 0) -> dict:
    keys = jax.random.split(jax.random.key(seed), 7)
    amplitudes = noise(keys[0], (ROWS, NBLK, BW), 1.0, 6.0, ((0, 256),))
    integrals = noise(keys[1], (SLOTS, BW, PAIRS), (NBLK * BW) ** -0.5, 0.015625, ((0, 64), (2, 4)))
    slot_block = draw_slot_block(jax.random.fold_in(keys[6], 71), 0)
    rest = noise(keys[3], (ROWS, PAIRS), 2.0, 12.0, ((0, 64), (1, 4)))
    occ_energy = jnp.clip(-2.0 + 1.5 * jax.random.uniform(keys[4], (ROWS,), jnp.float32) ** shard_levels(keys[4], (ROWS,), ((0, 64),), -0.2, 0.2), -2.0, -0.5)
    vir_energy = jnp.clip(0.5 + 2.5 * jax.random.uniform(keys[5], (PAIRS,), jnp.float32) ** shard_levels(keys[5], (PAIRS,), ((0, 4),), -0.2, 0.2), 0.5, 3.0)
    return dict(amplitudes=amplitudes, integrals=integrals, slot_block=slot_block, rest=rest, occ_energy=occ_energy, vir_energy=vir_energy)


def reference(amplitudes, integrals, slot_block, rest, occ_energy, vir_energy):
    slot_of = jnp.zeros((NBLK + 1,), jnp.int32).at[slot_block].set(jnp.arange(SLOTS, dtype=jnp.int32))

    def add_block(position, running):
        amp_block = lax.dynamic_index_in_dim(amplitudes, position, 1, keepdims=False)
        int_slab = lax.dynamic_index_in_dim(integrals, slot_of[position], 0, keepdims=False)
        return running + jnp.dot(amp_block, int_slab, preferred_element_type=jnp.float32)

    ladder = lax.fori_loop(0, NBLK, add_block, jnp.zeros((ROWS, PAIRS), jnp.float32))
    denominator = vir_energy[None, :] - occ_energy[:, None]
    return ((rest.astype(jnp.float32) + ladder) / denominator).astype(jnp.bfloat16)
```

```python
import jax
import jax.numpy as jnp
from jax import lax
from jax.sharding import Mesh, PartitionSpec as P

NZ, NX, NC, NY = 8, 4, 2, 4
CHUNKS = 2


def ring(size, shift):
    return [(i, (i + shift) % size) for i in range(size)]


def route(amp_rows, picker):
    rows, _, width = amp_rows.shape
    tiles = NZ * NX * NC
    with jax.named_scope("pick"):
        outgoing = jnp.einsum(
            "tsg,rgb->trsb", picker, amp_rows, preferred_element_type=jnp.float32
        ).astype(jnp.bfloat16)
    cap = outgoing.shape[2]
    with jax.named_scope("route"):
        routed = lax.all_to_all(outgoing, ("z", "x", "core"), 0, 0, tiled=True)
    routed = routed.reshape(NZ, NX, NC, rows, cap, width)
    return routed.transpose(3, 4, 2, 1, 0, 5).reshape(rows, cap, tiles, width)


def replicate(own):
    half = own.shape[0] // 2
    after = lax.ppermute(own, "y", ring(NY, -1))
    before = lax.ppermute(own, "y", ring(NY, 1))
    low = lax.ppermute(before[:half], "y", ring(NY, 1))
    high = lax.ppermute(after[half:], "y", ring(NY, -1))
    return after, low, high, before


def contract(rows, integrals):
    return jnp.einsum("rsme,sen->rmn", rows, integrals, preferred_element_type=jnp.float32)


def reduce_tiles(partial):
    core = lax.axis_index("core")
    rows, n = partial.shape[0], partial.shape[-1]
    with jax.named_scope("reduce_core"):
        away = lax.dynamic_index_in_dim(partial, 1 - core, 1, keepdims=False)
        kept = lax.dynamic_index_in_dim(partial, core, 1, keepdims=False)
        summed = kept + lax.ppermute(away, "core", ring(NC, 1))
    with jax.named_scope("reduce_zx"):
        outgoing = summed.transpose(2, 1, 0, 3).reshape(NZ * NX, rows, n)
        got = lax.all_to_all(outgoing, ("z", "x"), 0, 0, tiled=True)
        return jnp.sum(got, axis=0)


def per_device(amplitudes, integrals, slot_block, rest, occ_energy, vir_energy):
    nblocks = amplitudes.shape[1]
    cap = integrals.shape[0]
    n = integrals.shape[2]
    picker = (slot_block[:, None] == jnp.arange(nblocks, dtype=jnp.int32)[None, :]).astype(
        jnp.bfloat16
    )
    picker = picker.reshape(-1, cap, nblocks)
    step = amplitudes.shape[0] // CHUNKS
    pieces = []
    for c in range(CHUNKS):
        own = route(amplitudes[c * step : (c + 1) * step], picker)
        after, low, high, before = replicate(own)
        everything = [own, after, low, high, before]
        partial = jnp.concatenate([contract(rows, integrals) for rows in everything])
        partial = partial.reshape(-1, NC, NX, NZ, n)
        pieces.append(reduce_tiles(partial).reshape(NY, step, n))
    relative = jnp.concatenate(pieces, axis=1)
    k = lax.axis_index("y")
    doubled = jnp.concatenate([relative, relative], axis=0)
    ladder = lax.dynamic_slice_in_dim(doubled, (NY - k) % NY, NY, 0).reshape(rest.shape)
    denominator = vir_energy[None, :] - occ_energy[:, None]
    return ((rest.astype(jnp.float32) + ladder) / denominator).astype(jnp.bfloat16)


def solution(mesh):
    grid = Mesh(mesh.devices.reshape(NZ, NX, NC, NY), ("z", "x", "core", "y"))
    tile = ("z", "x", "core")
    in_specs = (
        P(tile + ("y",), None, None),
        P(tile, None, "y"),
        P(),
        P(tile, "y"),
        P(tile),
        P("y"),
    )
    return jax.shard_map(
        per_device, mesh=grid, in_specs=in_specs, out_specs=P(tile, "y"), check_vma=False
    )
```

```python
import jax
import jax.numpy as jnp
from jax import lax
from jax.sharding import Mesh, PartitionSpec as P

NZ, NX, NC, NY = 8, 4, 2, 4


def ring(size, shift):
    return [(i, (i + shift) % size) for i in range(size)]


def route(amp_rows, picker):
    rows, _, width = amp_rows.shape
    tiles = NZ * NX * NC
    with jax.named_scope("pick"):
        outgoing = jnp.einsum(
            "tsg,rgb->trsb", picker, amp_rows, preferred_element_type=jnp.float32
        ).astype(jnp.bfloat16)
    cap = outgoing.shape[2]
    with jax.named_scope("route"):
        routed = lax.all_to_all(outgoing, ("z", "x", "core"), 0, 0, tiled=True)
    routed = routed.reshape(NZ, NX, NC, rows, cap, width)
    return routed.transpose(3, 4, 2, 1, 0, 5).reshape(rows, cap, tiles, width)


def neighbours(own):
    return lax.ppermute(own, "y", ring(NY, -1)), lax.ppermute(own, "y", ring(NY, 1))


def opposite(after, before):
    half = after.shape[0] // 2
    low = lax.ppermute(before[:half], "y", ring(NY, 1))
    high = lax.ppermute(after[half:], "y", ring(NY, -1))
    return low, high


def contract(rows, integrals):
    partial = jnp.einsum("rsme,sen->rmn", rows, integrals, preferred_element_type=jnp.float32)
    return partial.reshape(rows.shape[0], NC, NX, NZ, -1)


def pick(array, index, axis):
    return lax.dynamic_index_in_dim(array, index, axis, keepdims=False)


def over_core(partials):
    core = lax.axis_index("core")
    with jax.named_scope("reduce_core"):
        away = jnp.concatenate([pick(part, 1 - core, 1) for part in partials])
        kept = jnp.concatenate([pick(part, core, 1) for part in partials])
        return kept + lax.ppermute(away, "core", ring(NC, 1))


def over_x(summed):
    x = lax.axis_index("x")
    with jax.named_scope("reduce_x"):
        total = pick(summed, x, 1)
        for shift in (1, 3, 2):
            total += lax.ppermute(pick(summed, (x + shift) % NX, 1), "x", ring(NX, shift))
        return total


def over_z(summed):
    with jax.named_scope("reduce_z"):
        outgoing = summed.transpose(1, 0, 2)
        return jnp.sum(lax.all_to_all(outgoing, "z", 0, 0, tiled=True), axis=0)


def per_device(amplitudes, integrals, slot_block, rest, occ_energy, vir_energy):
    nblocks = amplitudes.shape[1]
    cap = integrals.shape[0]
    n = integrals.shape[2]
    picker = (slot_block[:, None] == jnp.arange(nblocks, dtype=jnp.int32)[None, :]).astype(
        jnp.bfloat16
    )
    picker = picker.reshape(-1, cap, nblocks)
    step = amplitudes.shape[0] // 2

    own = lax.optimization_barrier(route(amplitudes[:step], picker))
    after, before = neighbours(own)
    low, high = opposite(after, before)
    later = route(amplitudes[step:], picker)
    later, low, high = lax.optimization_barrier((later, low, high))
    after_later, before_later = neighbours(later)
    parts = [contract(rows, integrals) for rows in (own, after, low, high, before)]
    first = over_core(parts)
    first, after_later, before_later = lax.optimization_barrier((first, after_later, before_later))

    low_later, high_later = opposite(after_later, before_later)
    first = over_z(over_x(first))
    sides = [contract(rows, integrals) for rows in (later, after_later, before_later)]
    sides = over_core(sides)
    first, sides, low_later, high_later = lax.optimization_barrier(
        (first, sides, low_later, high_later)
    )
    sides = over_x(sides)
    across = [contract(rows, integrals) for rows in (low_later, high_later)]
    across = over_x(over_core(across))
    second = over_z(jnp.concatenate([sides[: 2 * step], across, sides[2 * step :]]))
    first = first.reshape(NY, step, n)
    second = second.reshape(NY, step, n)

    relative = jnp.concatenate([first, second], axis=1)
    k = lax.axis_index("y")
    doubled = jnp.concatenate([relative, relative], axis=0)
    ladder = lax.dynamic_slice_in_dim(doubled, (NY - k) % NY, NY, 0).reshape(rest.shape)
    denominator = vir_energy[None, :] - occ_energy[:, None]
    return ((rest.astype(jnp.float32) + ladder) / denominator).astype(jnp.bfloat16)


def solution(mesh):
    grid = Mesh(mesh.devices.reshape(NZ, NX, NC, NY), ("z", "x", "core", "y"))
    tile = ("z", "x", "core")
    in_specs = (
        P(tile + ("y",), None, None),
        P(tile, None, "y"),
        P(),
        P(tile, "y"),
        P(tile),
        P("y"),
    )
    return jax.shard_map(
        per_device, mesh=grid, in_specs=in_specs, out_specs=P(tile, "y"), check_vma=False
    )
```

```python
import jax
import jax.numpy as jnp
from jax import lax
from jax.experimental import pallas as pl
from jax.experimental.pallas import tpu as pltpu
from jax.sharding import Mesh, PartitionSpec as P

NZ, NX, NC, NY = 8, 4, 2, 4
LANES = 128


def ring(size, shift):
    return [(i, (i + shift) % size) for i in range(size)]


def after_that(earlier, *values):
    return lax.optimization_barrier((earlier,) + values)[1:]


def gather_rows(amp_rows, picker):
    with jax.named_scope("pick"):
        return jnp.einsum(
            "tsg,rgb->trsb", picker, amp_rows, preferred_element_type=jnp.float32
        ).astype(jnp.bfloat16)


def route(outgoing):
    tiles, rows, cap, width = outgoing.shape
    with jax.named_scope("route"):
        routed = lax.all_to_all(outgoing, ("z", "x", "core"), 0, 0, tiled=True)
    routed = routed.reshape(NZ, NX, NC, rows, cap, width)
    routed = routed.transpose(3, 4, 2, 1, 0, 5).reshape(rows, cap, tiles, width)
    return lax.optimization_barrier(routed)


def neighbours(own):
    return lax.ppermute(own, "y", ring(NY, -1)), lax.ppermute(own, "y", ring(NY, 1))


def opposite(after, before):
    half = after.shape[0] // 2
    low = lax.ppermute(before[:half], "y", ring(NY, 1))
    high = lax.ppermute(after[half:], "y", ring(NY, -1))
    return low, high


def product(parts, integrals):
    cap, width, n = integrals.shape
    tiles = parts[0].shape[2]
    total = sum(part.shape[0] for part in parts)
    group = 2

    def body(*refs):
        *row_refs, integral_ref, out_ref = refs
        value = None
        for j in range(group):
            rows = jnp.concatenate([ref[:, j] for ref in row_refs]).reshape(total * tiles, width)
            term = jnp.dot(rows, integral_ref[j], preferred_element_type=jnp.float32)
            value = term if value is None else value + term
        value = value.reshape(total, tiles, n)

        @pl.when(pl.program_id(0) == 0)
        def _():
            out_ref[...] = value

        @pl.when(pl.program_id(0) > 0)
        def _():
            out_ref[...] += value

    return pl.pallas_call(
        body,
        grid=(cap // group,),
        out_shape=jax.ShapeDtypeStruct((total, tiles, n), jnp.float32),
        in_specs=[
            pl.BlockSpec((part.shape[0], group, tiles, width), lambda i: (0, i, 0, 0))
            for part in parts
        ]
        + [pl.BlockSpec((group, width, n), lambda i: (i, 0, 0))],
        out_specs=pl.BlockSpec((total, tiles, n), lambda i: (0, 0, 0)),
        compiler_params=pltpu.CompilerParams(vmem_limit_bytes=56 << 20),
        cost_estimate=pl.CostEstimate(
            flops=2 * total * tiles * cap * width * n,
            bytes_accessed=2 * cap * width * (n + total * tiles) + 4 * total * tiles * n,
            transcendentals=0,
        ),
        name="product",
    )(*parts, integrals)


def pick(array, index, axis):
    return lax.dynamic_index_in_dim(array, index, axis, keepdims=False)


def over_core(partial):
    core = lax.axis_index("core")
    rows, _, n = partial.shape
    partial = partial.reshape(rows, NC, NX, NZ, n)
    with jax.named_scope("reduce_core"):
        away = lax.ppermute(pick(partial, 1 - core, 1), "core", ring(NC, 1))
        summed = pick(partial, core, 1) + away
        summed = summed.reshape(rows, NX, NZ, n // LANES, LANES)
        return summed.transpose(2, 1, 0, 3, 4).reshape(NZ * NX, -1, LANES)


def over_zx(outgoing):
    with jax.named_scope("reduce_zx"):
        return jnp.sum(lax.all_to_all(outgoing, ("z", "x"), 0, 0, tiled=True), axis=0)


def per_device(amplitudes, integrals, slot_block, rest, occ_energy, vir_energy):
    nblocks = amplitudes.shape[1]
    cap = integrals.shape[0]
    n = integrals.shape[2]
    picker = (slot_block[:, None] == jnp.arange(nblocks, dtype=jnp.int32)[None, :]).astype(
        jnp.bfloat16
    )
    picker = picker.reshape(-1, cap, nblocks)
    step = amplitudes.shape[0] // 2

    outgoing = gather_rows(amplitudes[:step], picker)
    outgoing_later = gather_rows(amplitudes[step:], picker)
    own = route(outgoing)
    (outgoing_later,) = after_that(own, outgoing_later)
    after, before = neighbours(own)
    later = route(outgoing_later)
    low, high = opposite(*after_that(later, after, before))
    early = product([own, after, before, later], integrals)
    early = over_core(*after_that((low, high), early))
    after_later, before_later = neighbours(later)
    low_later, high_later = opposite(after_later, before_later)
    early = over_zx(early)
    low, high, low_later, high_later = after_that(early, low, high, low_later, high_later)
    late = [low, high, after_later, low_later, high_later, before_later]
    late = over_zx(over_core(product(late, integrals)))

    early = early.reshape(4, step, n)
    late = late.reshape(4, step, n)
    own, after, before, later = (early[i] for i in range(4))
    across, after_later, across_later, before_later = (late[i] for i in range(4))
    relative = jnp.concatenate(
        [own, later, after, after_later, across, across_later, before, before_later]
    ).reshape(NY, 2 * step, n)
    k = lax.axis_index("y")
    doubled = jnp.concatenate([relative, relative], axis=0)
    ladder = lax.dynamic_slice_in_dim(doubled, (NY - k) % NY, NY, 0).reshape(rest.shape)
    denominator = vir_energy[None, :] - occ_energy[:, None]
    return ((rest.astype(jnp.float32) + ladder) / denominator).astype(jnp.bfloat16)


def solution(mesh):
    grid = Mesh(mesh.devices.reshape(NZ, NX, NC, NY), ("z", "x", "core", "y"))
    tile = ("z", "x", "core")
    in_specs = (
        P(tile + ("y",), None, None),
        P(tile, None, "y"),
        P(),
        P(tile, "y"),
        P(tile),
        P("y"),
    )
    return jax.shard_map(
        per_device, mesh=grid, in_specs=in_specs, out_specs=P(tile, "y"), check_vma=False
    )
```

```python
import jax
import jax.numpy as jnp
from jax import lax
from jax.experimental import pallas as pl
from jax.experimental.pallas import tpu as pltpu
from jax.sharding import Mesh, PartitionSpec as P

NZ, NX, NC, NY = 8, 4, 2, 4


def ring(size, shift):
    return [(i, (i + shift) % size) for i in range(size)]


def after_that(earlier, *values):
    return lax.optimization_barrier((earlier,) + values)[1:]


def gather_rows(amp_rows, picker):
    with jax.named_scope("pick"):
        return jnp.einsum(
            "tsg,rgb->trsb", picker, amp_rows, preferred_element_type=jnp.float32
        ).astype(jnp.bfloat16)


def route(outgoing):
    tiles, rows, cap, width = outgoing.shape
    with jax.named_scope("route"):
        routed = lax.all_to_all(outgoing, ("z", "x", "core"), 0, 0, tiled=True)
    routed = routed.reshape(NZ, NX, NC, rows, cap, width)
    routed = routed.transpose(3, 4, 2, 1, 0, 5).reshape(rows, cap, tiles, width)
    return lax.optimization_barrier(routed)


def neighbours(own):
    return lax.ppermute(own, "y", ring(NY, -1)), lax.ppermute(own, "y", ring(NY, 1))


def opposite(after, before):
    half = after.shape[0] // 2
    low = lax.ppermute(before[:half], "y", ring(NY, 1))
    high = lax.ppermute(after[half:], "y", ring(NY, -1))
    return low, high


def product(parts, gathered, integrals):
    cap, width, n = integrals.shape
    group = 4
    tiles = parts[0].shape[2]
    near = tiles // NC
    place = jnp.stack([lax.axis_index("core"), lax.axis_index("y")]).astype(jnp.int32)
    operands = list(parts)
    specs = [
        pl.BlockSpec((part.shape[0], group, tiles, width), lambda i, place: (0, i, 0, 0))
        for part in parts
    ]
    total = sum(part.shape[0] for part in parts)
    if gathered is not None:
        rows = gathered.shape[1]
        for shift in (1, 2, 3):
            operands.append(gathered)
            specs.append(
                pl.BlockSpec(
                    (None, rows, group, tiles, width),
                    lambda i, place, shift=shift: ((place[1] + shift) % NY, 0, i, 0, 0),
                )
            )
            total += rows
    steps = cap // group

    def body(place_ref, *refs):
        *row_refs, integral_ref, kept_ref, away_ref, sum_ref = refs
        step = pl.program_id(0)
        value = None
        for j in range(group):
            rows = jnp.concatenate([ref[:, j] for ref in row_refs]).reshape(total * tiles, width)
            term = jnp.dot(rows, integral_ref[j], preferred_element_type=jnp.float32)
            value = term if value is None else value + term
        value = value.reshape(total, tiles, n)

        @pl.when(step == 0)
        def _():
            sum_ref[...] = value

        @pl.when(jnp.logical_and(step > 0, step < steps - 1))
        def _():
            sum_ref[...] += value

        @pl.when(step == steps - 1)
        def _():
            sums = sum_ref[...] + value

            def put(first_ref, second_ref):
                for r in range(total):
                    first_ref[:, r, :] = sums[r, :near]
                    second_ref[:, r, :] = sums[r, near:]

            @pl.when(place_ref[0] == 0)
            def _():
                put(kept_ref, away_ref)

            @pl.when(place_ref[0] == 1)
            def _():
                put(away_ref, kept_ref)

    out = jax.ShapeDtypeStruct((near, total, n), jnp.float32)
    out_spec = pl.BlockSpec((near, total, n), lambda i, place: (0, 0, 0))
    return pl.pallas_call(
        body,
        grid_spec=pltpu.PrefetchScalarGridSpec(
            num_scalar_prefetch=1,
            grid=(steps,),
            in_specs=specs + [pl.BlockSpec((group, width, n), lambda i, place: (i, 0, 0))],
            out_specs=[out_spec, out_spec],
            scratch_shapes=[pltpu.VMEM((total, tiles, n), jnp.float32)],
        ),
        out_shape=[out, out],
        compiler_params=pltpu.CompilerParams(vmem_limit_bytes=56 << 20),
        cost_estimate=pl.CostEstimate(
            flops=2 * total * tiles * cap * width * n,
            bytes_accessed=2 * cap * width * (n + total * tiles) + 4 * total * tiles * n,
            transcendentals=0,
        ),
        name="product",
    )(place, *operands, integrals)


def over_core(sums):
    kept, away = sums
    with jax.named_scope("reduce_core"):
        return kept + lax.ppermute(away, "core", ring(NC, 1))


def over_xz(outgoing):
    with jax.named_scope("reduce_xz"):
        return jnp.sum(lax.all_to_all(outgoing, ("x", "z"), 0, 0, tiled=True), axis=0)


def per_device(amplitudes, integrals, slot_block, rest, occ_energy, vir_energy):
    nblocks = amplitudes.shape[1]
    cap = integrals.shape[0]
    n = integrals.shape[2]
    picker = (slot_block[:, None] == jnp.arange(nblocks, dtype=jnp.int32)[None, :]).astype(
        jnp.bfloat16
    )
    picker = picker.reshape(-1, cap, nblocks)
    step = amplitudes.shape[0] // 2

    outgoing = gather_rows(amplitudes[:step], picker)
    outgoing_later = gather_rows(amplitudes[step:], picker)
    own = route(outgoing)
    (outgoing_later,) = after_that(own, outgoing_later)
    after, before = neighbours(own)
    later = route(outgoing_later)
    (later,) = after_that((after, before), later)
    with jax.named_scope("replicate_later"):
        gathered = lax.all_gather(later, "y", axis=0, tiled=False)
    low, high = opposite(*after_that(later, after, before))
    early = over_core(product([own, after, before, later], None, integrals))
    low, high = after_that(early, low, high)
    early = over_xz(early)
    late = over_xz(over_core(product([low, high], gathered, integrals)))

    early = early.reshape(4, step, n)
    late = late.reshape(4, step, n)
    own, after, before, later = (early[i] for i in range(4))
    across, after_later, across_later, before_later = (late[i] for i in range(4))
    relative = jnp.concatenate(
        [own, later, after, after_later, across, across_later, before, before_later]
    ).reshape(NY, 2 * step, n)
    k = lax.axis_index("y")
    doubled = jnp.concatenate([relative, relative], axis=0)
    ladder = lax.dynamic_slice_in_dim(doubled, (NY - k) % NY, NY, 0).reshape(rest.shape)
    denominator = vir_energy[None, :] - occ_energy[:, None]
    return ((rest.astype(jnp.float32) + ladder) / denominator).astype(jnp.bfloat16)


def solution(mesh):
    grid = Mesh(mesh.devices.reshape(NZ, NX, NC, NY), ("z", "x", "core", "y"))
    tile = ("z", "x", "core")
    in_specs = (
        P(tile + ("y",), None, None),
        P(tile, None, "y"),
        P(),
        P(tile, "y"),
        P(tile),
        P("y"),
    )
    return jax.shard_map(
        per_device, mesh=grid, in_specs=in_specs, out_specs=P(tile, "y"), check_vma=False
    )
```

```python
import jax
import jax.numpy as jnp
from jax import lax
from jax.experimental import pallas as pl
from jax.experimental.pallas import tpu as pltpu
from jax.sharding import Mesh, PartitionSpec as P

NZ, NX, NC, NY = 8, 4, 2, 4
ROWS = 8


def ring(size, shift):
    return [(i, (i + shift) % size) for i in range(size)]


def after_that(earlier, *values):
    return lax.optimization_barrier((earlier,) + values)[1:]


def gather_rows(amp_rows, picker):
    with jax.named_scope("pick"):
        return jnp.einsum(
            "tsg,rgb->trsb", picker, amp_rows, preferred_element_type=jnp.float32
        ).astype(jnp.bfloat16)


def route(outgoing):
    tiles, rows, cap, width = outgoing.shape
    with jax.named_scope("route"):
        routed = lax.all_to_all(outgoing, ("z", "x", "core"), 0, 0, tiled=True)
    routed = routed.reshape(NZ, NX, NC, rows, cap, width)
    routed = routed.transpose(3, 4, 2, 1, 0, 5).reshape(rows, cap, tiles, width)
    return lax.optimization_barrier(routed)


def neighbours(own):
    return lax.ppermute(own, "y", ring(NY, -1)), lax.ppermute(own, "y", ring(NY, 1))


def opposite(after, before):
    half = after.shape[0] // 2
    low = lax.ppermute(before[:half], "y", ring(NY, 1))
    high = lax.ppermute(after[half:], "y", ring(NY, -1))
    return low, high


def product(parts, integrals, base=None):
    cap, width, n = integrals.shape
    group = 4
    tiles = parts[0].shape[2]
    near = tiles // NC
    place = lax.axis_index("core").astype(jnp.int32).reshape(1)
    total = sum(part.shape[0] for part in parts)
    offset = ROWS - total if base is not None else 0
    steps = cap // group

    def body(place_ref, *refs):
        *refs, integral_ref, kept_ref, away_ref, sum_ref = refs
        base_refs, row_refs = refs[: len(refs) - len(parts)], refs[len(refs) - len(parts) :]
        step = pl.program_id(0)
        value = None
        for j in range(group):
            rows = jnp.concatenate([ref[:, j] for ref in row_refs]).reshape(total * tiles, width)
            term = jnp.dot(rows, integral_ref[j], preferred_element_type=jnp.float32)
            value = term if value is None else value + term
        value = value.reshape(total, tiles, n)

        @pl.when(step == 0)
        def _():
            sum_ref[...] = value

        @pl.when(jnp.logical_and(step > 0, step < steps - 1))
        def _():
            sum_ref[...] += value

        @pl.when(step == steps - 1)
        def _():
            sums = sum_ref[...] + value
            for base_ref, out_ref in zip(base_refs, (kept_ref, away_ref)):
                out_ref[...] = base_ref[...]

            def put(first_ref, second_ref):
                for r in range(total):
                    first_ref[:, offset + r, :] = sums[r, :near]
                    second_ref[:, offset + r, :] = sums[r, near:]

            @pl.when(place_ref[0] == 0)
            def _():
                put(kept_ref, away_ref)

            @pl.when(place_ref[0] == 1)
            def _():
                put(away_ref, kept_ref)

    out = jax.ShapeDtypeStruct((near, ROWS, n), jnp.float32)
    out_spec = pl.BlockSpec((near, ROWS, n), lambda i, place: (0, 0, 0))
    row_specs = [
        pl.BlockSpec((part.shape[0], group, tiles, width), lambda i, place: (0, i, 0, 0))
        for part in parts
    ]
    base = [] if base is None else list(base)
    return pl.pallas_call(
        body,
        grid_spec=pltpu.PrefetchScalarGridSpec(
            num_scalar_prefetch=1,
            grid=(steps,),
            in_specs=[out_spec] * len(base)
            + row_specs
            + [pl.BlockSpec((group, width, n), lambda i, place: (i, 0, 0))],
            out_specs=[out_spec, out_spec],
            scratch_shapes=[pltpu.VMEM((total, tiles, n), jnp.float32)],
        ),
        out_shape=[out, out],
        compiler_params=pltpu.CompilerParams(vmem_limit_bytes=56 << 20),
        cost_estimate=pl.CostEstimate(
            flops=2 * total * tiles * cap * width * n,
            bytes_accessed=2 * cap * width * (n + total * tiles) + 4 * total * tiles * n,
            transcendentals=0,
        ),
        name="product",
    )(place, *base, *parts, integrals)


def over_core(sums):
    kept, away = sums
    with jax.named_scope("reduce_core"):
        return kept + lax.ppermute(away, "core", ring(NC, 1))


def over_xz(outgoing):
    with jax.named_scope("reduce_xz"):
        return jnp.sum(lax.all_to_all(outgoing, ("x", "z"), 0, 0, tiled=True), axis=0)


def per_device(amplitudes, integrals, slot_block, rest, occ_energy, vir_energy):
    nblocks = amplitudes.shape[1]
    cap = integrals.shape[0]
    n = integrals.shape[2]
    picker = (slot_block[:, None] == jnp.arange(nblocks, dtype=jnp.int32)[None, :]).astype(
        jnp.bfloat16
    )
    picker = picker.reshape(-1, cap, nblocks)
    step = amplitudes.shape[0] // 2

    outgoing = gather_rows(amplitudes[:step], picker)
    outgoing_later = gather_rows(amplitudes[step:], picker)
    own = route(outgoing)
    (outgoing_later,) = after_that(own, outgoing_later)
    after, before = neighbours(own)
    later = route(outgoing_later)
    (later,) = after_that((after, before), later)
    low, high = opposite(*after_that(later, after, before))
    after_later, before_later = neighbours(later)
    low_later, high_later = opposite(after_later, before_later)
    kept, away = product([own, after, before, later], integrals)
    low, high, away = lax.optimization_barrier((low, high, away))
    early = over_core((kept, away))
    early = over_xz(early)
    late = product([low, high, after_later, before_later], integrals)
    late = product([low_later, high_later], integrals, late)
    late = over_xz(over_core(late))

    early = early.reshape(4, step, n)
    late = late.reshape(4, step, n)
    own, after, before, later = (early[i] for i in range(4))
    across, after_later, before_later, across_later = (late[i] for i in range(4))
    relative = jnp.concatenate(
        [own, later, after, after_later, across, across_later, before, before_later]
    ).reshape(NY, 2 * step, n)
    k = lax.axis_index("y")
    doubled = jnp.concatenate([relative, relative], axis=0)
    ladder = lax.dynamic_slice_in_dim(doubled, (NY - k) % NY, NY, 0).reshape(rest.shape)
    denominator = vir_energy[None, :] - occ_energy[:, None]
    return ((rest.astype(jnp.float32) + ladder) / denominator).astype(jnp.bfloat16)


def solution(mesh):
    grid = Mesh(mesh.devices.reshape(NZ, NX, NC, NY), ("z", "x", "core", "y"))
    tile = ("z", "x", "core")
    in_specs = (
        P(tile + ("y",), None, None),
        P(tile, None, "y"),
        P(),
        P(tile, "y"),
        P(tile),
        P("y"),
    )
    return jax.shard_map(
        per_device, mesh=grid, in_specs=in_specs, out_specs=P(tile, "y"), check_vma=False
    )
```

```python
import jax
import jax.numpy as jnp
from jax import lax
from jax.experimental import pallas as pl
from jax.experimental.pallas import tpu as pltpu
from jax.sharding import Mesh, PartitionSpec as P

NZ, NX, NC, NY = 8, 4, 2, 4


def ring(size, shift):
    return [(i, (i + shift) % size) for i in range(size)]


def after_that(earlier, *values):
    return lax.optimization_barrier((earlier,) + values)[1:]


def gather_rows(amp_rows, picker):
    with jax.named_scope("pick"):
        return jnp.einsum(
            "tsg,rgb->trsb", picker, amp_rows, preferred_element_type=jnp.float32
        ).astype(jnp.bfloat16)


def route(outgoing):
    tiles, rows, cap, width = outgoing.shape
    with jax.named_scope("route"):
        routed = lax.all_to_all(outgoing, ("z", "x", "core"), 0, 0, tiled=True)
    routed = routed.reshape(NZ, NX, NC, rows, cap, width)
    routed = [
        routed[:, :, :, r].transpose(3, 2, 1, 0, 4).reshape(1, cap, tiles, width)
        for r in range(rows)
    ]
    return lax.optimization_barrier(routed)


def forward(row):
    return lax.ppermute(row, "y", ring(NY, 1))


def backward(row):
    return lax.ppermute(row, "y", ring(NY, -1))


def product(parts, integrals):
    cap, width, n = integrals.shape
    group = 4
    tiles = parts[0].shape[2]
    near = tiles // NC
    place = lax.axis_index("core").astype(jnp.int32).reshape(1)
    total = sum(part.shape[0] for part in parts)
    steps = cap // group

    def body(place_ref, *refs):
        *row_refs, integral_ref, kept_ref, away_ref, sum_ref = refs
        step = pl.program_id(0)
        value = None
        for j in range(group):
            rows = jnp.concatenate([ref[:, j] for ref in row_refs]).reshape(total * tiles, width)
            term = jnp.dot(rows, integral_ref[j], preferred_element_type=jnp.float32)
            value = term if value is None else value + term
        value = value.reshape(total, tiles, n)

        @pl.when(step == 0)
        def _():
            sum_ref[...] = value

        @pl.when(jnp.logical_and(step > 0, step < steps - 1))
        def _():
            sum_ref[...] += value

        @pl.when(step == steps - 1)
        def _():
            sums = sum_ref[...] + value

            def put(first_ref, second_ref):
                for r in range(total):
                    first_ref[:, r, :] = sums[r, :near]
                    second_ref[:, r, :] = sums[r, near:]

            @pl.when(place_ref[0] == 0)
            def _():
                put(kept_ref, away_ref)

            @pl.when(place_ref[0] == 1)
            def _():
                put(away_ref, kept_ref)

    out = jax.ShapeDtypeStruct((near, total, n), jnp.float32)
    out_spec = pl.BlockSpec((near, total, n), lambda i, place: (0, 0, 0))
    row_specs = [
        pl.BlockSpec((part.shape[0], group, tiles, width), lambda i, place: (0, i, 0, 0))
        for part in parts
    ]
    return pl.pallas_call(
        body,
        grid_spec=pltpu.PrefetchScalarGridSpec(
            num_scalar_prefetch=1,
            grid=(steps,),
            in_specs=row_specs
            + [pl.BlockSpec((group, width, n), lambda i, place: (i, 0, 0))],
            out_specs=[out_spec, out_spec],
            scratch_shapes=[pltpu.VMEM((total, tiles, n), jnp.float32)],
        ),
        out_shape=[out, out],
        compiler_params=pltpu.CompilerParams(vmem_limit_bytes=56 << 20),
        cost_estimate=pl.CostEstimate(
            flops=2 * total * tiles * cap * width * n,
            bytes_accessed=2 * cap * width * (n + total * tiles) + 4 * total * tiles * n,
            transcendentals=0,
        ),
        name="product",
    )(place, *parts, integrals)


def over_core(sums):
    kept, away = sums
    with jax.named_scope("reduce_core"):
        return kept + lax.ppermute(away, "core", ring(NC, 1))


def over_xz(outgoing):
    with jax.named_scope("reduce_xz"):
        return jnp.sum(lax.all_to_all(outgoing, ("x", "z"), 0, 0, tiled=True), axis=0)


def over_x_then_z(outgoing, earlier):
    x = lax.axis_index("x")
    outgoing = outgoing.reshape(NX, NZ, *outgoing.shape[1:])
    with jax.named_scope("reduce_x"):
        total = lax.dynamic_index_in_dim(outgoing, x, 0, keepdims=False)
        for shift in (1, 3, 2):
            away = lax.dynamic_index_in_dim(outgoing, (x + shift) % NX, 0, keepdims=False)
            total += lax.ppermute(away, "x", ring(NX, shift))
    with jax.named_scope("reduce_z"):
        (total,) = after_that(earlier, total)
        return jnp.sum(lax.all_to_all(total, "z", 0, 0, tiled=True), axis=0)


def per_device(amplitudes, integrals, slot_block, rest, occ_energy, vir_energy):
    nblocks = amplitudes.shape[1]
    cap = integrals.shape[0]
    n = integrals.shape[2]
    picker = (slot_block[:, None] == jnp.arange(nblocks, dtype=jnp.int32)[None, :]).astype(
        jnp.bfloat16
    )
    picker = picker.reshape(-1, cap, nblocks)
    step = amplitudes.shape[0] // 2

    outgoing = gather_rows(amplitudes[:step], picker)
    outgoing_later = gather_rows(amplitudes[step:], picker)
    own = route(outgoing)
    (outgoing_later,) = after_that(own, outgoing_later)
    after = [backward(row) for row in own]
    before = [forward(row) for row in own]
    later = route(outgoing_later)
    (later,) = after_that((after, before), later)
    across = [forward(before[0]), backward(after[1])]
    before_later = [forward(later[0])]
    after_later = [backward(later[1])]
    kept, away = product([*own, *after, *before, *later], integrals)
    (away,) = after_that((across, before_later, after_later), away)
    early = over_core((kept, away))
    (across,) = after_that(early, across)
    early = over_xz(early)

    across_later = [forward(before_later[0]), backward(after_later[0])]
    before_later = [before_later[0], forward(later[1])]
    after_later = [backward(later[0]), after_later[0]]
    late = product([*across, *after_later, *before_later, *across_later], integrals)
    late = over_x_then_z(over_core(late), early)

    early = early.reshape(4, step, n)
    late = late.reshape(4, step, n)
    own, after, before, later = (early[i] for i in range(4))
    across, after_later, before_later, across_later = (late[i] for i in range(4))
    relative = jnp.concatenate(
        [own, later, after, after_later, across, across_later, before, before_later]
    ).reshape(NY, 2 * step, n)
    k = lax.axis_index("y")
    doubled = jnp.concatenate([relative, relative], axis=0)
    ladder = lax.dynamic_slice_in_dim(doubled, (NY - k) % NY, NY, 0).reshape(rest.shape)
    denominator = vir_energy[None, :] - occ_energy[:, None]
    return ((rest.astype(jnp.float32) + ladder) / denominator).astype(jnp.bfloat16)


def solution(mesh):
    grid = Mesh(mesh.devices.reshape(NZ, NX, NC, NY), ("z", "x", "core", "y"))
    tile = ("z", "x", "core")
    in_specs = (
        P(tile + ("y",), None, None),
        P(tile, None, "y"),
        P(),
        P(tile, "y"),
        P(tile),
        P("y"),
    )
    return jax.shard_map(
        per_device, mesh=grid, in_specs=in_specs, out_specs=P(tile, "y"), check_vma=False
    )
```

```python
import jax
import jax.numpy as jnp
from jax import lax
from jax.experimental import pallas as pl
from jax.experimental.pallas import tpu as pltpu
from jax.sharding import Mesh, PartitionSpec as P

NZ, NX, NC, NY = 8, 4, 2, 4


def ring(size, shift):
    return [(i, (i + shift) % size) for i in range(size)]


def after_that(earlier, *values):
    return lax.optimization_barrier((earlier,) + values)[1:]


def gather_rows(amp_rows, picker):
    with jax.named_scope("pick"):
        return jnp.einsum(
            "tsg,rgb->trsb", picker, amp_rows, preferred_element_type=jnp.float32
        ).astype(jnp.bfloat16)


def route(outgoing):
    tiles, rows, cap, width = outgoing.shape
    with jax.named_scope("route"):
        routed = lax.all_to_all(outgoing, ("z", "x", "core"), 0, 0, tiled=True)
    routed = routed.reshape(NZ, NX, NC, rows, cap, width)
    routed = [
        routed[:, :, :, r].transpose(3, 2, 1, 0, 4).reshape(1, cap, tiles, width)
        for r in range(rows)
    ]
    return lax.optimization_barrier(routed)


def forward(row):
    return lax.ppermute(row, "y", ring(NY, 1))


def backward(row):
    return lax.ppermute(row, "y", ring(NY, -1))


def product(parts, integrals):
    cap, width, n = integrals.shape
    group = 4
    tiles = parts[0].shape[2]
    near = tiles // NC
    place = lax.axis_index("core").astype(jnp.int32).reshape(1)
    total = sum(part.shape[0] for part in parts)
    steps = cap // group

    def body(place_ref, *refs):
        *row_refs, integral_ref, kept_ref, away_ref, sum_ref = refs
        step = pl.program_id(0)
        value = None
        for j in range(group):
            rows = jnp.concatenate([ref[:, j] for ref in row_refs]).reshape(total * tiles, width)
            term = jnp.dot(rows, integral_ref[j], preferred_element_type=jnp.float32)
            value = term if value is None else value + term
        value = value.reshape(total, tiles, n)

        @pl.when(step == 0)
        def _():
            sum_ref[...] = value

        @pl.when(jnp.logical_and(step > 0, step < steps - 1))
        def _():
            sum_ref[...] += value

        @pl.when(step == steps - 1)
        def _():
            sums = sum_ref[...] + value

            def put(first_ref, second_ref):
                for r in range(total):
                    first_ref[:, r, :] = sums[r, :near]
                    second_ref[:, r, :] = sums[r, near:]

            @pl.when(place_ref[0] == 0)
            def _():
                put(kept_ref, away_ref)

            @pl.when(place_ref[0] == 1)
            def _():
                put(away_ref, kept_ref)

    out = jax.ShapeDtypeStruct((near, total, n), jnp.float32)
    out_spec = pl.BlockSpec((near, total, n), lambda i, place: (0, 0, 0))
    row_specs = [
        pl.BlockSpec((part.shape[0], group, tiles, width), lambda i, place: (0, i, 0, 0))
        for part in parts
    ]
    return pl.pallas_call(
        body,
        grid_spec=pltpu.PrefetchScalarGridSpec(
            num_scalar_prefetch=1,
            grid=(steps,),
            in_specs=row_specs
            + [pl.BlockSpec((group, width, n), lambda i, place: (i, 0, 0))],
            out_specs=[out_spec, out_spec],
            scratch_shapes=[pltpu.VMEM((total, tiles, n), jnp.float32)],
        ),
        out_shape=[out, out],
        compiler_params=pltpu.CompilerParams(vmem_limit_bytes=56 << 20),
        cost_estimate=pl.CostEstimate(
            flops=2 * total * tiles * cap * width * n,
            bytes_accessed=2 * cap * width * (n + total * tiles) + 4 * total * tiles * n,
            transcendentals=0,
        ),
        name="product",
    )(place, *parts, integrals)


def over_core(sums):
    kept, away = sums
    with jax.named_scope("reduce_core"):
        return kept + lax.ppermute(away, "core", ring(NC, 1))


def over_xz(outgoing):
    with jax.named_scope("reduce_xz"):
        return jnp.sum(lax.all_to_all(outgoing, ("x", "z"), 0, 0, tiled=True), axis=0)


def over_axis(outgoing, axis):
    size = lax.axis_size(axis)
    place = lax.axis_index(axis)
    total = lax.dynamic_index_in_dim(outgoing, place, 0, keepdims=False)
    for shift in range(1, size):
        away = lax.dynamic_index_in_dim(outgoing, (place + shift) % size, 0, keepdims=False)
        total += lax.ppermute(away, axis, ring(size, shift))
    return total


def over_x_then_z(outgoing, earlier):
    outgoing = outgoing.reshape(NX, NZ, *outgoing.shape[1:])
    with jax.named_scope("reduce_x"):
        outgoing = over_axis(outgoing, "x")
    (outgoing,) = after_that(earlier, outgoing)
    with jax.named_scope("reduce_z"):
        return over_axis(outgoing, "z")


def per_device(amplitudes, integrals, slot_block, rest, occ_energy, vir_energy):
    nblocks = amplitudes.shape[1]
    cap = integrals.shape[0]
    picker = (slot_block[:, None] == jnp.arange(nblocks, dtype=jnp.int32)[None, :]).astype(
        jnp.bfloat16
    )
    picker = picker.reshape(-1, cap, nblocks)
    cuts = [(0, 2), (2, 3), (3, 4)]
    outgoing = [gather_rows(amplitudes[low:high], picker) for low, high in cuts]

    own = route(outgoing[0])
    (outgoing[1],) = after_that(own, outgoing[1])
    after = [backward(row) for row in own]
    before = [forward(row) for row in own]
    across = [forward(before[0]), backward(after[1])]

    own_later = route(outgoing[1])
    (outgoing[2],) = after_that(own_later, outgoing[2])
    (own_later,) = after_that((after, before), own_later)
    after_later = [backward(row) for row in own_later]
    before_later = [forward(row) for row in own_later]
    across_later = [forward(before_later[0])]
    kept, away = product([*own, *after, *across, *before], integrals)

    last = route(outgoing[2])
    (away,) = after_that(last, away)
    (last,) = after_that((after_later, before_later), last)
    own_later += last
    after_later += [backward(row) for row in last]
    before_later += [forward(row) for row in last]
    across_later += [backward(after_later[1])]

    early = over_core((kept, away))
    (across_later,) = after_that(early, across_later)
    early = over_xz(early)
    late = product([*own_later, *after_later, *across_later, *before_later], integrals)
    late = over_x_then_z(over_core(late), early)

    n = integrals.shape[2]
    relative = jnp.concatenate([early.reshape(NY, 2, n), late.reshape(NY, 2, n)], axis=1)
    k = lax.axis_index("y")
    doubled = jnp.concatenate([relative, relative], axis=0)
    ladder = lax.dynamic_slice_in_dim(doubled, (NY - k) % NY, NY, 0).reshape(rest.shape)
    denominator = vir_energy[None, :] - occ_energy[:, None]
    return ((rest.astype(jnp.float32) + ladder) / denominator).astype(jnp.bfloat16)


def solution(mesh):
    grid = Mesh(mesh.devices.reshape(NZ, NX, NC, NY), ("z", "x", "core", "y"))
    tile = ("z", "x", "core")
    in_specs = (
        P(tile + ("y",), None, None),
        P(tile, None, "y"),
        P(),
        P(tile, "y"),
        P(tile),
        P("y"),
    )
    return jax.shard_map(
        per_device, mesh=grid, in_specs=in_specs, out_specs=P(tile, "y"), check_vma=False
    )
```

```python
import jax
import jax.numpy as jnp
from jax import lax
from jax.experimental import pallas as pl
from jax.experimental.pallas import tpu as pltpu
from jax.sharding import Mesh, PartitionSpec as P

NZ, NX, NC, NY = 8, 4, 2, 4


def ring(size, shift):
    return [(i, (i + shift) % size) for i in range(size)]


def after_that(earlier, *values):
    return lax.optimization_barrier((earlier,) + values)[1:]


def gather_rows(amp_rows, picker):
    with jax.named_scope("pick"):
        return jnp.einsum(
            "tsg,rgb->trsb", picker, amp_rows, preferred_element_type=jnp.float32
        ).astype(jnp.bfloat16)


def route(outgoing):
    tiles, rows, cap, width = outgoing.shape
    with jax.named_scope("route"):
        routed = lax.all_to_all(outgoing, ("z", "x", "core"), 0, 0, tiled=True)
    routed = routed.reshape(NZ, NX, NC, rows, cap, width)
    routed = [
        routed[:, :, :, r].transpose(3, 2, 1, 0, 4).reshape(1, cap, tiles, width)
        for r in range(rows)
    ]
    return lax.optimization_barrier(routed)


def forward(row):
    return lax.ppermute(row, "y", ring(NY, 1))


def backward(row):
    return lax.ppermute(row, "y", ring(NY, -1))


def product(parts, integrals):
    cap, width, n = integrals.shape
    group = 4
    tiles = parts[0].shape[2]
    near = tiles // NC
    place = lax.axis_index("core").astype(jnp.int32).reshape(1)
    total = sum(part.shape[0] for part in parts)
    steps = cap // group

    def body(place_ref, *refs):
        *row_refs, integral_ref, kept_ref, away_ref, sum_ref = refs
        step = pl.program_id(0)
        value = None
        for j in range(group):
            rows = jnp.concatenate([ref[:, j] for ref in row_refs]).reshape(total * tiles, width)
            term = jnp.dot(rows, integral_ref[j], preferred_element_type=jnp.float32)
            value = term if value is None else value + term
        value = value.reshape(total, tiles, n)

        @pl.when(step == 0)
        def _():
            sum_ref[...] = value

        @pl.when(jnp.logical_and(step > 0, step < steps - 1))
        def _():
            sum_ref[...] += value

        @pl.when(step == steps - 1)
        def _():
            sums = sum_ref[...] + value

            def put(first_ref, second_ref):
                for r in range(total):
                    first_ref[:, r, :] = sums[r, :near]
                    second_ref[:, r, :] = sums[r, near:]

            @pl.when(place_ref[0] == 0)
            def _():
                put(kept_ref, away_ref)

            @pl.when(place_ref[0] == 1)
            def _():
                put(away_ref, kept_ref)

    out = jax.ShapeDtypeStruct((near, total, n), jnp.float32)
    out_spec = pl.BlockSpec((near, total, n), lambda i, place: (0, 0, 0))
    row_specs = [
        pl.BlockSpec((part.shape[0], group, tiles, width), lambda i, place: (0, i, 0, 0))
        for part in parts
    ]
    return pl.pallas_call(
        body,
        grid_spec=pltpu.PrefetchScalarGridSpec(
            num_scalar_prefetch=1,
            grid=(steps,),
            in_specs=row_specs
            + [pl.BlockSpec((group, width, n), lambda i, place: (i, 0, 0))],
            out_specs=[out_spec, out_spec],
            scratch_shapes=[pltpu.VMEM((total, tiles, n), jnp.float32)],
        ),
        out_shape=[out, out],
        compiler_params=pltpu.CompilerParams(vmem_limit_bytes=56 << 20),
        cost_estimate=pl.CostEstimate(
            flops=2 * total * tiles * cap * width * n,
            bytes_accessed=2 * cap * width * (n + total * tiles) + 4 * total * tiles * n,
            transcendentals=0,
        ),
        name="product",
    )(place, *parts, integrals)


def over_core(sums):
    kept, away = sums
    with jax.named_scope("reduce_core"):
        return kept + lax.ppermute(away, "core", ring(NC, 1))


def over_xz(outgoing):
    with jax.named_scope("reduce_xz"):
        return jnp.sum(lax.all_to_all(outgoing, ("x", "z"), 0, 0, tiled=True), axis=0)


def over_x_then_z(outgoing, earlier):
    x = lax.axis_index("x")
    outgoing = outgoing.reshape(NX, NZ, *outgoing.shape[1:])
    with jax.named_scope("reduce_x"):
        total = lax.dynamic_index_in_dim(outgoing, x, 0, keepdims=False)
        for shift in (1, 3, 2):
            away = lax.dynamic_index_in_dim(outgoing, (x + shift) % NX, 0, keepdims=False)
            total += lax.ppermute(away, "x", ring(NX, shift))
    with jax.named_scope("reduce_z"):
        (total,) = after_that(earlier, total)
        return jnp.sum(lax.all_to_all(total, "z", 0, 0, tiled=True), axis=0)


def per_device(amplitudes, integrals, slot_block, rest, occ_energy, vir_energy):
    nblocks = amplitudes.shape[1]
    cap = integrals.shape[0]
    n = integrals.shape[2]
    picker = (slot_block[:, None] == jnp.arange(nblocks, dtype=jnp.int32)[None, :]).astype(
        jnp.bfloat16
    )
    picker = picker.reshape(-1, cap, nblocks)
    step = amplitudes.shape[0] // 2

    outgoing = gather_rows(amplitudes[:step], picker)
    outgoing_later = gather_rows(amplitudes[step:], picker)
    own = route(outgoing)
    (outgoing_later,) = after_that(own, outgoing_later)
    after = [backward(row) for row in own]
    before = [forward(row) for row in own]
    later = route(outgoing_later)
    (later,) = after_that((after, before), later)
    across = [forward(before[0]), backward(after[1])]
    before_later = [forward(row) for row in later]
    after_later = [backward(row) for row in later]
    kept, away = product([*own, *after, *before, *later], integrals)
    (away,) = after_that((across, before_later, after_later), away)
    early = over_core((kept, away))
    (across,) = after_that(early, across)
    early = over_xz(early)

    across_later = [forward(before_later[0]), backward(after_later[1])]
    late = product([*across, *after_later, *before_later, *across_later], integrals)
    late = over_x_then_z(over_core(late), early)

    early = early.reshape(4, step, n)
    late = late.reshape(4, step, n)
    own, after, before, later = (early[i] for i in range(4))
    across, after_later, before_later, across_later = (late[i] for i in range(4))
    relative = jnp.concatenate(
        [own, later, after, after_later, across, across_later, before, before_later]
    ).reshape(NY, 2 * step, n)
    k = lax.axis_index("y")
    doubled = jnp.concatenate([relative, relative], axis=0)
    ladder = lax.dynamic_slice_in_dim(doubled, (NY - k) % NY, NY, 0).reshape(rest.shape)
    denominator = vir_energy[None, :] - occ_energy[:, None]
    return ((rest.astype(jnp.float32) + ladder) / denominator).astype(jnp.bfloat16)


def solution(mesh):
    grid = Mesh(mesh.devices.reshape(NZ, NX, NC, NY), ("z", "x", "core", "y"))
    tile = ("z", "x", "core")
    in_specs = (
        P(tile + ("y",), None, None),
        P(tile, None, "y"),
        P(),
        P(tile, "y"),
        P(tile),
        P("y"),
    )
    return jax.shard_map(
        per_device, mesh=grid, in_specs=in_specs, out_specs=P(tile, "y"), check_vma=False
    )
```

```python
import jax
import jax.numpy as jnp
from jax import lax
from jax.experimental import pallas as pl
from jax.experimental.pallas import tpu as pltpu
from jax.sharding import Mesh, PartitionSpec as P

NZ, NX, NC, NY = 8, 4, 2, 4
LANES = 128


def ring(size, shift):
    return [(i, (i + shift) % size) for i in range(size)]


def after_that(earlier, *values):
    return lax.optimization_barrier((earlier,) + values)[1:]


def gather_rows(amp_rows, picker):
    with jax.named_scope("pick"):
        return jnp.einsum(
            "tsg,rgb->trsb", picker, amp_rows, preferred_element_type=jnp.float32
        ).astype(jnp.bfloat16)


def route(outgoing):
    tiles, rows, cap, width = outgoing.shape
    with jax.named_scope("route"):
        routed = lax.all_to_all(outgoing, ("z", "x", "core"), 0, 0, tiled=True)
    routed = routed.reshape(NZ, NX, NC, rows, cap, width)
    routed = [
        routed[:, :, :, r].transpose(3, 2, 1, 0, 4).reshape(1, cap, tiles, width)
        for r in range(rows)
    ]
    return lax.optimization_barrier(routed)


def forward(row):
    return lax.ppermute(row, "y", ring(NY, 1))


def backward(row):
    return lax.ppermute(row, "y", ring(NY, -1))


def product(parts, integrals):
    cap, width, n = integrals.shape
    group = 4
    tiles = parts[0].shape[2]
    near = tiles // NC
    place = lax.axis_index("core").astype(jnp.int32).reshape(1)
    total = sum(part.shape[0] for part in parts)
    steps = cap // group

    def body(place_ref, *refs):
        *row_refs, integral_ref, kept_ref, away_ref, sum_ref = refs
        step = pl.program_id(0)
        value = None
        for j in range(group):
            rows = jnp.concatenate([ref[:, j] for ref in row_refs]).reshape(total * tiles, width)
            term = jnp.dot(rows, integral_ref[j], preferred_element_type=jnp.float32)
            value = term if value is None else value + term
        value = value.reshape(total, tiles, n)

        @pl.when(step == 0)
        def _():
            sum_ref[...] = value

        @pl.when(jnp.logical_and(step > 0, step < steps - 1))
        def _():
            sum_ref[...] += value

        @pl.when(step == steps - 1)
        def _():
            sums = sum_ref[...] + value

            def put(first_ref, second_ref):
                for r in range(total):
                    for c in range(n // LANES):
                        piece = sums[r, :, c * LANES : (c + 1) * LANES]
                        first_ref[:, r * (n // LANES) + c, :] = piece[:near]
                        second_ref[:, r * (n // LANES) + c, :] = piece[near:]

            @pl.when(place_ref[0] == 0)
            def _():
                put(kept_ref, away_ref)

            @pl.when(place_ref[0] == 1)
            def _():
                put(away_ref, kept_ref)

    out = jax.ShapeDtypeStruct((near, total * n // LANES, LANES), jnp.float32)
    out_spec = pl.BlockSpec(out.shape, lambda i, place: (0, 0, 0))
    row_specs = [
        pl.BlockSpec((part.shape[0], group, tiles, width), lambda i, place: (0, i, 0, 0))
        for part in parts
    ]
    return pl.pallas_call(
        body,
        grid_spec=pltpu.PrefetchScalarGridSpec(
            num_scalar_prefetch=1,
            grid=(steps,),
            in_specs=row_specs
            + [pl.BlockSpec((group, width, n), lambda i, place: (i, 0, 0))],
            out_specs=[out_spec, out_spec],
            scratch_shapes=[pltpu.VMEM((total, tiles, n), jnp.float32)],
        ),
        out_shape=[out, out],
        compiler_params=pltpu.CompilerParams(vmem_limit_bytes=56 << 20),
        cost_estimate=pl.CostEstimate(
            flops=2 * total * tiles * cap * width * n,
            bytes_accessed=2 * cap * width * (n + total * tiles) + 4 * total * tiles * n,
            transcendentals=0,
        ),
        name="product",
    )(place, *parts, integrals)


def over_core(sums):
    kept, away = sums
    with jax.named_scope("reduce_core"):
        return kept + lax.ppermute(away, "core", ring(NC, 1))


def over_xz(outgoing):
    with jax.named_scope("reduce_xz"):
        return jnp.sum(lax.all_to_all(outgoing, ("x", "z"), 0, 0, tiled=True), axis=0)


def over_x_then_z(outgoing, earlier):
    x = lax.axis_index("x")
    outgoing = outgoing.reshape(NX, NZ, *outgoing.shape[1:])
    with jax.named_scope("reduce_x"):
        total = lax.dynamic_index_in_dim(outgoing, x, 0, keepdims=False)
        for shift in (1, 3, 2):
            away = lax.dynamic_index_in_dim(outgoing, (x + shift) % NX, 0, keepdims=False)
            total += lax.ppermute(away, "x", ring(NX, shift))
    with jax.named_scope("reduce_z"):
        (total,) = after_that(earlier, total)
        return jnp.sum(lax.all_to_all(total, "z", 0, 0, tiled=True), axis=0)


def per_device(amplitudes, integrals, slot_block, rest, occ_energy, vir_energy):
    nblocks = amplitudes.shape[1]
    cap = integrals.shape[0]
    n = integrals.shape[2]
    picker = (slot_block[:, None] == jnp.arange(nblocks, dtype=jnp.int32)[None, :]).astype(
        jnp.bfloat16
    )
    picker = picker.reshape(-1, cap, nblocks)
    step = amplitudes.shape[0] // 2

    outgoing = gather_rows(amplitudes[:step], picker)
    outgoing_later = gather_rows(amplitudes[step:], picker)
    own = route(outgoing)
    (outgoing_later,) = after_that(own, outgoing_later)
    after = [backward(row) for row in own]
    before = [forward(row) for row in own]
    later = route(outgoing_later)
    (later,) = after_that((after, before), later)
    across = [forward(before[0]), backward(after[1])]
    before_later = [forward(row) for row in later]
    after_later = [backward(row) for row in later]
    kept, away = product([*own, *after, *before, *later, across[0]], integrals)
    (away,) = after_that((before_later, after_later, across), away)
    early = over_core((kept, away))

    across_later = [forward(before_later[0]), backward(after_later[1])]
    sides = after_that(early, *after_later, *before_later)
    early = over_xz(early)
    late = product([across[1], *sides, *across_later], integrals)
    late = over_x_then_z(over_core(late), early)

    sums = jnp.concatenate([early, late]).reshape(8, step, n)
    own, after, before, later, across, after_later, before_later, across_later = sums
    relative = jnp.concatenate(
        [own, later, after, after_later, across, across_later, before, before_later]
    ).reshape(NY, 2 * step, n)
    k = lax.axis_index("y")
    doubled = jnp.concatenate([relative, relative], axis=0)
    ladder = lax.dynamic_slice_in_dim(doubled, (NY - k) % NY, NY, 0).reshape(rest.shape)
    denominator = vir_energy[None, :] - occ_energy[:, None]
    return ((rest.astype(jnp.float32) + ladder) / denominator).astype(jnp.bfloat16)


def solution(mesh):
    grid = Mesh(mesh.devices.reshape(NZ, NX, NC, NY), ("z", "x", "core", "y"))
    tile = ("z", "x", "core")
    in_specs = (
        P(tile + ("y",), None, None),
        P(tile, None, "y"),
        P(),
        P(tile, "y"),
        P(tile),
        P("y"),
    )
    return jax.shard_map(
        per_device, mesh=grid, in_specs=in_specs, out_specs=P(tile, "y"), check_vma=False
    )
```

```python
import jax
import jax.numpy as jnp
from jax import lax
from jax.experimental import pallas as pl
from jax.experimental.pallas import tpu as pltpu
from jax.sharding import Mesh, PartitionSpec as P

NZ, NX, NC, NY = 8, 4, 2, 4
LANES = 128


def ring(size, shift):
    return [(i, (i + shift) % size) for i in range(size)]


def after_that(earlier, *values):
    return lax.optimization_barrier((earlier,) + values)[1:]


def gather_rows(amp_rows, picker):
    with jax.named_scope("pick"):
        return jnp.einsum(
            "tsg,rgb->trsb", picker, amp_rows, preferred_element_type=jnp.float32
        ).astype(jnp.bfloat16)


def route(outgoing):
    tiles, rows, cap, width = outgoing.shape
    with jax.named_scope("route"):
        routed = lax.all_to_all(outgoing, ("z", "x", "core"), 0, 0, tiled=True)
    routed = routed.reshape(NZ, NX, NC, rows, cap, width)
    routed = [
        routed[:, :, :, r].transpose(3, 2, 1, 0, 4).reshape(1, cap, tiles, width)
        for r in range(rows)
    ]
    return lax.optimization_barrier(routed)


def forward(row):
    return lax.ppermute(row, "y", ring(NY, 1))


def backward(row):
    return lax.ppermute(row, "y", ring(NY, -1))


def product(parts, integrals):
    cap, width, n = integrals.shape
    group = 4
    tiles = parts[0].shape[2]
    near = tiles // NC
    place = lax.axis_index("core").astype(jnp.int32).reshape(1)
    total = sum(part.shape[0] for part in parts)
    steps = cap // group

    def body(place_ref, *refs):
        *row_refs, integral_ref, kept_ref, away_ref, sum_ref = refs
        step = pl.program_id(0)
        value = None
        for j in range(group):
            rows = jnp.concatenate([ref[:, j] for ref in row_refs]).reshape(total * tiles, width)
            term = jnp.dot(rows, integral_ref[j], preferred_element_type=jnp.float32)
            value = term if value is None else value + term
        value = value.reshape(total, tiles, n)

        @pl.when(step == 0)
        def _():
            sum_ref[...] = value

        @pl.when(jnp.logical_and(step > 0, step < steps - 1))
        def _():
            sum_ref[...] += value

        @pl.when(step == steps - 1)
        def _():
            sums = sum_ref[...] + value

            def put(first_ref, second_ref):
                for r in range(total):
                    for c in range(n // LANES):
                        piece = sums[r, :, c * LANES : (c + 1) * LANES]
                        first_ref[:, r * (n // LANES) + c, :] = piece[:near]
                        second_ref[:, r * (n // LANES) + c, :] = piece[near:]

            @pl.when(place_ref[0] == 0)
            def _():
                put(kept_ref, away_ref)

            @pl.when(place_ref[0] == 1)
            def _():
                put(away_ref, kept_ref)

    out = jax.ShapeDtypeStruct((near, total * n // LANES, LANES), jnp.float32)
    out_spec = pl.BlockSpec(out.shape, lambda i, place: (0, 0, 0))
    row_specs = [
        pl.BlockSpec((part.shape[0], group, tiles, width), lambda i, place: (0, i, 0, 0))
        for part in parts
    ]
    return pl.pallas_call(
        body,
        grid_spec=pltpu.PrefetchScalarGridSpec(
            num_scalar_prefetch=1,
            grid=(steps,),
            in_specs=row_specs
            + [pl.BlockSpec((group, width, n), lambda i, place: (i, 0, 0))],
            out_specs=[out_spec, out_spec],
            scratch_shapes=[pltpu.VMEM((total, tiles, n), jnp.float32)],
        ),
        out_shape=[out, out],
        compiler_params=pltpu.CompilerParams(vmem_limit_bytes=56 << 20),
        cost_estimate=pl.CostEstimate(
            flops=2 * total * tiles * cap * width * n,
            bytes_accessed=2 * cap * width * (n + total * tiles) + 4 * total * tiles * n,
            transcendentals=0,
        ),
        name="product",
    )(place, *parts, integrals)


def over_core(sums):
    kept, away = sums
    with jax.named_scope("reduce_core"):
        return kept + lax.ppermute(away, "core", ring(NC, 1))


def over_xz(outgoing):
    with jax.named_scope("reduce_xz"):
        return jnp.sum(lax.all_to_all(outgoing, ("x", "z"), 0, 0, tiled=True), axis=0)


def over_x_then_z(outgoing, earlier):
    x = lax.axis_index("x")
    outgoing = outgoing.reshape(NX, NZ, *outgoing.shape[1:])
    with jax.named_scope("reduce_x"):
        total = lax.dynamic_index_in_dim(outgoing, x, 0, keepdims=False)
        for shift in (2, 1, 3):
            away = lax.dynamic_index_in_dim(outgoing, (x + shift) % NX, 0, keepdims=False)
            total += lax.ppermute(away, "x", ring(NX, shift))
    with jax.named_scope("reduce_z"):
        (total,) = after_that(earlier, total)
        return jnp.sum(lax.all_to_all(total, "z", 0, 0, tiled=True), axis=0)


def per_device(amplitudes, integrals, slot_block, rest, occ_energy, vir_energy):
    nblocks = amplitudes.shape[1]
    cap = integrals.shape[0]
    n = integrals.shape[2]
    picker = (slot_block[:, None] == jnp.arange(nblocks, dtype=jnp.int32)[None, :]).astype(
        jnp.bfloat16
    )
    picker = picker.reshape(-1, cap, nblocks)
    step = amplitudes.shape[0] // 2

    outgoing = gather_rows(amplitudes[:step], picker)
    outgoing_later = gather_rows(amplitudes[step:], picker)
    own = route(outgoing)
    (outgoing_later,) = after_that(own, outgoing_later)
    after = [backward(row) for row in own]
    before = [forward(row) for row in own]
    later = route(outgoing_later)
    (later,) = after_that((after, before), later)
    across = [forward(before[0]), backward(after[1])]
    before_later = [forward(row) for row in later]
    after_later = [backward(row) for row in later]
    kept, away = product([*own, *after, *before, *later, across[0]], integrals)
    (away,) = after_that((before_later, after_later, across), away)
    early = over_core((kept, away))

    across_later = [forward(before_later[0]), backward(after_later[1])]
    sides = after_that(early, *after_later, *before_later)
    early = over_xz(early)
    late = product([across[1], *sides, *across_later], integrals)
    late = over_x_then_z(over_core(late), early)

    sums = jnp.concatenate([early, late]).reshape(8, step, n)
    own, after, before, later, across, after_later, before_later, across_later = sums
    relative = jnp.concatenate(
        [own, later, after, after_later, across, across_later, before, before_later]
    ).reshape(NY, 2 * step, n)
    k = lax.axis_index("y")
    doubled = jnp.concatenate([relative, relative], axis=0)
    ladder = lax.dynamic_slice_in_dim(doubled, (NY - k) % NY, NY, 0).reshape(rest.shape)
    denominator = vir_energy[None, :] - occ_energy[:, None]
    return ((rest.astype(jnp.float32) + ladder) / denominator).astype(jnp.bfloat16)


def solution(mesh):
    grid = Mesh(mesh.devices.reshape(NZ, NX, NC, NY), ("z", "x", "core", "y"))
    tile = ("z", "x", "core")
    in_specs = (
        P(tile + ("y",), None, None),
        P(tile, None, "y"),
        P(),
        P(tile, "y"),
        P(tile),
        P("y"),
    )
    return jax.shard_map(
        per_device, mesh=grid, in_specs=in_specs, out_specs=P(tile, "y"), check_vma=False
    )
```
